1024 devices in a mesh: row: 32 (over z), col: 32 (over y, x, core).
Axes of the slice: x: 4, y: 4, z: 32, core: 2. Of those that a mesh axis runs over, the one named last changes fastest.
Arguments:
- leaf_source: float32 [32, 32, 2, 16, 128], P('row', 'col'), may hold values from -6 to 6
- leaf_pivot: float32 [8192, 8192], P('row', 'col'), may hold values from -0.375 to 0.375
- leaf_update: float32 [16384, 8192], P('row', 'col'), may hold values from -0.09375 to 0.09375
- leaf_targets: int32 [32, 32, 4], P('row', 'col'), may hold values from 0 to 191, as said below
- root_source: float32 [32, 32, 2, 64], P('row', 'col'), may hold values from -6 to 6
- middle_source: float32 [32, 32, 4, 64], P('row', 'col'), may hold values from -6 to 6
- lower_source: float32 [32, 32, 4, 128], P('row', 'col'), may hold values from -6 to 6
- root_pivot: float32 [8192, 8192], P('row', 'col'), may hold values from -0.0625 to 0.0625
- middle_pivot: float32 [8192, 16384], P('row', 'col'), may hold values from -0.0625 to 0.0625
- lower_pivot: float32 [16384, 16384], P('row', 'col'), may hold values from -0.0625 to 0.0625
- middle_update: float32 [4096, 16384], P('row', 'col'), may hold values from -0.09375 to 0.09375
- lower_update: float32 [8192, 16384], P('row', 'col'), may hold values from -0.09375 to 0.09375
- middle_targets: int32 [2, 32], replicated, may hold values from 0 to 63, as said below
- lower_targets: int32 [4, 32], replicated, may hold values from 0 to 127, as said below
Outputs:
- root_solution: float32 [32, 32, 2, 16, 128], P('row', 'col')
- middle_solution: float32 [32, 32, 4, 16, 128], P('row', 'col')
- lower_solution: float32 [32, 32, 4, 16, 128], P('row', 'col')
- leaf_solution: float32 [32, 32, 2, 16, 128], P('row', 'col')
The draws below stay inside these ranges and needn't reach their ends.
Inputs may be any that keep to these rules, and one draw needn't show every extreme that they name: `middle_targets`: the 32 entries of a row are different root blocks. `lower_targets`: the 32 entries of a row are different chain blocks of the root and the parent front. `leaf_targets`: the 4 entries of a device are different chain blocks.
All inputs are finite; a program needn't handle non-finite values.
Results may differ from the reference program's by a relative error of at most 0.00013.
Values sent between devices are 32-bit elements; how exact they have to be, the bound alone decides.
A program may use at most 32 MiB of HBM per device.

```python
import jax
import jax.numpy as jnp
from jax import lax

BLOCK = 128
SOURCES = 16
SEP_BLOCKS = 64
UPD_BLOCKS = 32
LEAF_BLOCKS = 2
LEAF_UPDATE = 4
SEP_ROWS = 8192
LEAF_ROWS = 256
N_ROW = 32
N_COL = 32


def distinct_rows(key, row_count, pool_size, taken_count):
    keys = jax.random.split(key, row_count)
    return jax.vmap(lambda one_key: jax.random.permutation(one_key, pool_size)[:taken_count])(keys).astype(jnp.int32)


def draw_middle_targets(key, part):
    key = jax.random.fold_in(key, 11)
    return distinct_rows(key, 2, SEP_BLOCKS, UPD_BLOCKS)


def draw_lower_targets(key, part):
    key = jax.random.fold_in(key, 12)
    return distinct_rows(key, 4, 2 * SEP_BLOCKS, UPD_BLOCKS)


def draw_leaf_targets(key, part):
    key = jax.random.fold_in(key, 13)
    return distinct_rows(key, N_ROW * N_COL, 3 * SEP_BLOCKS, LEAF_UPDATE).reshape(N_ROW, N_COL, LEAF_UPDATE)


def levels(rng, shape, shards, smallest, largest):
    def one(position, parts):
        steps = jax.random.uniform(jax.random.fold_in(jax.random.fold_in(rng, 6), position), (parts,), jnp.float32, smallest / len(shards), largest / len(shards))
        return jnp.repeat(jnp.exp(steps), shape[position] // parts).reshape((-1,) + (1,) * (len(shape) - position - 1))

    level = one(*shards[0])
    for cut in shards[1:]:
        level = level * one(*cut)
    return level


def normal_values(stream_key, dims, deviation, reach, cuts=(), kind=jnp.bfloat16):
    result = jax.random.normal(stream_key, dims, jnp.float32) * deviation
    if len(cuts) > 0:
        result = levels(stream_key, dims, cuts, -0.22, 0.18) * result
    return jnp.clip(result, min=-reach, max=reach).astype(kind)


def setup_inputs(seed: int = 0) -> dict:
    seeds = jax.random.split(jax.random.key(seed), 15)
    leaf_source = normal_values(seeds[0], (N_ROW, N_COL, LEAF_BLOCKS, SOURCES, BLOCK), 1.0, 6.0, ((0, 32), (1, 32)), jnp.float32)
    leaf_pivot = normal_values(seeds[1], (N_ROW * LEAF_ROWS, N_COL * LEAF_ROWS), LEAF_ROWS ** -0.5, 0.375, ((0, 32), (1, 32)), jnp.float32)
    leaf_update = normal_values(seeds[2], (N_ROW * LEAF_UPDATE * BLOCK, N_COL * LEAF_ROWS), (16 * LEAF_ROWS) ** -0.5, 0.09375, ((0, 32), (1, 32)), jnp.float32)
    leaf_targets = draw_leaf_targets(jax.random.fold_in(seeds[14], 71), 0)
    root_source = normal_values(seeds[4], (N_ROW, N_COL, SEP_BLOCKS // N_COL, SOURCES * BLOCK // N_ROW), 1.0, 6.0, ((0, 32), (1, 32)), jnp.float32)
    middle_source = normal_values(seeds[5], (N_ROW, N_COL, 2 * SEP_BLOCKS // N_COL, SOURCES * BLOCK // N_ROW), 1.0, 6.0, ((0, 32), (1, 32)), jnp.float32)
    lower_source = normal_values(seeds[6], (N_ROW, N_COL, 2 * SEP_BLOCKS // N_COL, 2 * SOURCES * BLOCK // N_ROW), 1.0, 6.0, ((0, 32), (1, 32)), jnp.float32)
    root_pivot = normal_values(seeds[7], (SEP_ROWS, SEP_ROWS), SEP_ROWS ** -0.5, 0.0625, ((0, 32), (1, 32)), jnp.float32)
    middle_pivot = normal_values(seeds[8], (SEP_ROWS, 2 * SEP_ROWS), SEP_ROWS ** -0.5, 0.0625, ((0, 32), (1, 32)), jnp.float32)
    lower_pivot = normal_values(seeds[9], (2 * SEP_ROWS, 2 * SEP_ROWS), SEP_ROWS ** -0.5, 0.0625, ((0, 32), (1, 32)), jnp.float32)
    middle_update = normal_values(seeds[10], (UPD_BLOCKS * BLOCK, 2 * SEP_ROWS), (UPD_BLOCKS * BLOCK) ** -0.5, 0.09375, ((0, 32), (1, 32)), jnp.float32)
    lower_update = normal_values(seeds[11], (2 * UPD_BLOCKS * BLOCK, 2 * SEP_ROWS), (UPD_BLOCKS * BLOCK) ** -0.5, 0.09375, ((0, 32), (1, 32)), jnp.float32)
    middle_targets = draw_middle_targets(jax.random.fold_in(seeds[14], 71), 0)
    lower_targets = draw_lower_targets(jax.random.fold_in(seeds[14], 71), 0)
    return dict(leaf_source=leaf_source, leaf_pivot=leaf_pivot, leaf_update=leaf_update, leaf_targets=leaf_targets, root_source=root_source, middle_source=middle_source, lower_source=lower_source, root_pivot=root_pivot, middle_pivot=middle_pivot, lower_pivot=lower_pivot, middle_update=middle_update, lower_update=lower_update, middle_targets=middle_targets, lower_targets=lower_targets)


precise = lax.Precision.HIGHEST


def assemble(tiles, group_rows, group_cols, front_blocks):
    row_groups = N_ROW // group_rows
    col_groups = N_COL // group_cols
    shaped = tiles.reshape(row_groups, group_rows, front_blocks // group_rows, BLOCK, col_groups, group_cols, SEP_BLOCKS // group_cols, BLOCK)
    shaped = shaped.transpose(4, 0, 2, 1, 3, 6, 5, 7)
    return shaped.reshape(row_groups * col_groups, front_blocks * BLOCK, SEP_ROWS)


def assemble_sources(tiles, group_rows, group_cols):
    row_groups = N_ROW // group_rows
    col_groups = N_COL // group_cols
    shaped = tiles.reshape(row_groups, group_rows, col_groups, group_cols, SEP_BLOCKS // group_cols, SOURCES * BLOCK // group_rows)
    shaped = shaped.transpose(2, 0, 4, 3, 1, 5)
    return shaped.reshape(row_groups * col_groups, SEP_BLOCKS, SOURCES, BLOCK)


def spread_out(fronts, group_rows, group_cols):
    row_groups = N_ROW // group_rows
    col_groups = N_COL // group_cols
    col_tiles = SEP_BLOCKS // group_cols
    shaped = fronts.reshape(col_groups, row_groups, col_tiles, group_cols, SOURCES, BLOCK)
    shaped = shaped.transpose(1, 0, 3, 2, 4, 5)[:, None]
    shaped = jnp.broadcast_to(shaped, (row_groups, group_rows, col_groups, group_cols, col_tiles, SOURCES, BLOCK))
    return shaped.reshape(N_ROW, N_COL, col_tiles, SOURCES, BLOCK)


def to_flat(blocks):
    return blocks.transpose(0, 2, 1, 3).reshape(blocks.shape[0], SOURCES, blocks.shape[1] * BLOCK)


def from_flat(flat):
    return flat.reshape(flat.shape[0], SOURCES, flat.shape[2] // BLOCK, BLOCK).transpose(0, 2, 1, 3)


def forward_product(matrices, blocks):
    return jnp.einsum("fmn,fkn->fkm", matrices, to_flat(blocks), precision=precise)


def backward_product(matrices, flat):
    return jnp.einsum("fmn,fkm->fkn", matrices, flat, precision=precise)


def reference(leaf_source, leaf_pivot, leaf_update, leaf_targets, root_source, middle_source, lower_source, root_pivot, middle_pivot, lower_pivot, middle_update, lower_update, middle_targets, lower_targets):
    half_rows = N_ROW // 2
    half_cols = N_COL // 2
    root_inv = assemble(root_pivot, N_ROW, N_COL, SEP_BLOCKS)
    middle_inv = assemble(middle_pivot, N_ROW, half_cols, SEP_BLOCKS)
    lower_inv = assemble(lower_pivot, half_rows, half_cols, SEP_BLOCKS)
    middle_ops = assemble(middle_update, N_ROW, half_cols, UPD_BLOCKS)
    lower_ops = assemble(lower_update, half_rows, half_cols, UPD_BLOCKS)
    root_src = assemble_sources(root_source, N_ROW, N_COL)
    middle_src = assemble_sources(middle_source, N_ROW, half_cols)
    lower_src = assemble_sources(lower_source, half_rows, half_cols)
    row_ids = jnp.arange(N_ROW, dtype=jnp.int32)[:, None]
    col_ids = jnp.arange(N_COL, dtype=jnp.int32)[None, :]
    middle_front = col_ids // half_cols + 0 * row_ids
    lower_front = 2 * (col_ids // half_cols) + row_ids // half_rows
    leaf_global = jnp.where(leaf_targets < SEP_BLOCKS, leaf_targets,
                            jnp.where(leaf_targets < 2 * SEP_BLOCKS,
                                      leaf_targets + middle_front[:, :, None] * SEP_BLOCKS,
                                      leaf_targets + SEP_BLOCKS + lower_front[:, :, None] * SEP_BLOCKS)).astype(jnp.int32)
    leaf_inv = leaf_pivot.reshape(N_ROW, LEAF_ROWS, N_COL, LEAF_ROWS).transpose(0, 2, 1, 3)
    leaf_ops = leaf_update.reshape(N_ROW, LEAF_UPDATE * BLOCK, N_COL, LEAF_ROWS).transpose(0, 2, 1, 3)
    leaf_vector = leaf_source.transpose(0, 1, 3, 2, 4).reshape(N_ROW, N_COL, SOURCES, LEAF_ROWS)
    leaf_forward = jnp.einsum("rcmn,rckn->rckm", leaf_inv, leaf_vector, precision=precise)
    leaf_send = jnp.einsum("rcmn,rckn->rckm", leaf_ops, leaf_vector, precision=precise)
    leaf_send = leaf_send.reshape(N_ROW, N_COL, SOURCES, LEAF_UPDATE, BLOCK).transpose(0, 1, 3, 2, 4)
    total_blocks = 7 * SEP_BLOCKS
    contrib = jax.ops.segment_sum(leaf_send.reshape(N_ROW * N_COL * LEAF_UPDATE, SOURCES, BLOCK), leaf_global.reshape(-1), num_segments=total_blocks)
    lower_input = lower_src - contrib[3 * SEP_BLOCKS:].reshape(4, SEP_BLOCKS, SOURCES, BLOCK)
    lower_forward = forward_product(lower_inv, lower_input)
    lower_send = from_flat(forward_product(lower_ops, lower_input))
    parent_ids = (jnp.arange(4, dtype=jnp.int32) // 2)[:, None]
    lower_global = jnp.where(lower_targets < SEP_BLOCKS, lower_targets, lower_targets + parent_ids * SEP_BLOCKS).astype(jnp.int32)
    contrib = contrib + jax.ops.segment_sum(lower_send.reshape(4 * UPD_BLOCKS, SOURCES, BLOCK), lower_global.reshape(-1), num_segments=total_blocks)
    middle_input = middle_src - contrib[SEP_BLOCKS:3 * SEP_BLOCKS].reshape(2, SEP_BLOCKS, SOURCES, BLOCK)
    middle_forward = forward_product(middle_inv, middle_input)
    middle_send = from_flat(forward_product(middle_ops, middle_input))
    contrib = contrib + jax.ops.segment_sum(middle_send.reshape(2 * UPD_BLOCKS, SOURCES, BLOCK), middle_targets.reshape(-1), num_segments=total_blocks)
    root_input = root_src - contrib[:SEP_BLOCKS][None]
    root_forward = forward_product(root_inv, root_input)
    root_x = from_flat(backward_product(root_inv, root_forward))
    root_chain = root_x.reshape(SEP_BLOCKS, SOURCES, BLOCK)
    middle_fetch = root_chain[middle_targets]
    middle_x = from_flat(backward_product(middle_inv, middle_forward) - backward_product(middle_ops, to_flat(middle_fetch)))
    upper_chain = jnp.concatenate([root_chain, middle_x.reshape(2 * SEP_BLOCKS, SOURCES, BLOCK)], axis=0)
    lower_fetch = upper_chain[lower_global]
    lower_x = from_flat(backward_product(lower_inv, lower_forward) - backward_product(lower_ops, to_flat(lower_fetch)))
    full_chain = jnp.concatenate([upper_chain, lower_x.reshape(4 * SEP_BLOCKS, SOURCES, BLOCK)], axis=0)
    leaf_fetch = full_chain[leaf_global].transpose(0, 1, 3, 2, 4).reshape(N_ROW, N_COL, SOURCES, LEAF_UPDATE * BLOCK)
    leaf_x = jnp.einsum("rcmn,rckm->rckn", leaf_inv, leaf_forward, precision=precise) - jnp.einsum("rcmn,rckm->rckn", leaf_ops, leaf_fetch, precision=precise)
    leaf_x = leaf_x.reshape(N_ROW, N_COL, SOURCES, LEAF_BLOCKS, BLOCK).transpose(0, 1, 3, 2, 4)
    return (spread_out(root_x, N_ROW, N_COL), spread_out(middle_x, N_ROW, half_cols), spread_out(lower_x, half_rows, half_cols), leaf_x)
```

```python
import jax
import jax.numpy as jnp
from jax import lax
from jax.experimental import pallas as pl
from jax.experimental.pallas import tpu as pltpu
from jax.sharding import PartitionSpec as P

MESH = pl.DeviceIdType.MESH
F32 = jnp.float32
BF16 = jnp.bfloat16

PHASES = {
    "targets": ("row16", 1),
    "leaf_send": ("row16", 4),
    "middle_source": ("row32", 2),
    "root_source": ("row32", 1),
    "low_sum": ("col16", 4),
    "mid_sum": ("col16", 4),
    "root_sum": ("col32", 2),
    "low_input": ("row16", 4),
    "mid_base": ("row32", 4),
    "root_base": ("row32", 2),
    "low_update": ("col16", 2),
    "low_product": ("col16", 4),
    "low_forward": ("col16", 4),
    "low_spread": ("row32", 2),
    "mid_input": ("col16", 4),
    "mid_update": ("col16", 1),
    "mid_product": ("col16", 2),
    "mid_forward": ("col16", 2),
    "mid_spread": ("row32", 1),
    "root_input": ("col32", 2),
    "root_product": ("col32", 1),
    "root_forward": ("col32", 1),
    "root_terms": ("col32", 2),
    "mid_fetch": ("row32", 1),
    "mid_fetched": ("col16", 1),
    "root_rows": ("row32", 1),
    "root_out": ("row32", 1),
    "root_chain": ("col32", 2),
    "mid_terms": ("col16", 4),
    "low_fetch": ("row32", 2),
    "low_fetched": ("col16", 2),
    "mid_rows": ("row32", 2),
    "mid_out": ("row32", 2),
    "mid_chain": ("col16", 4),
    "low_rows": ("row16", 4),
    "low_chain": ("col16", 4),
    "low_out": ("row16", 4),
    "leaf_fetch": ("row16", 4),
}
NAMES = list(PHASES)
COUNT = {"row16": 16, "row32": 32, "col16": 16, "col32": 32}

SOURCES_OF = {
    "targets": 1,
    "leaf_send": 64,
    "middle_source": 2,
    "root_source": 1,
    "low_sum": 64,
    "mid_sum": 64,
    "root_sum": 64,
    "low_input": 4,
    "mid_base": 4,
    "root_base": 2,
    "low_update": 32,
    "low_product": 64,
    "low_forward": 4,
    "low_spread": 2,
    "mid_input": 64,
    "mid_update": 16,
    "mid_product": 32,
    "mid_forward": 2,
    "mid_spread": 1,
    "root_input": 64,
    "root_product": 32,
    "root_forward": 1,
    "root_terms": 32,
    "mid_fetch": 32,
    "mid_fetched": 1,
    "root_rows": 32,
    "root_out": 1,
    "root_chain": 2,
    "mid_terms": 64,
    "low_fetch": 64,
    "low_fetched": 2,
    "mid_rows": 64,
    "mid_out": 2,
    "mid_chain": 4,
    "low_rows": 64,
    "low_chain": 4,
    "low_out": 4,
    "leaf_fetch": 64,
}

MATRICES = {
    "leaf_update": (512, 256),
    "leaf_pivot": (256, 256),
    "lower_update": (256, 512),
    "lower_pivot": (512, 512),
    "middle_update": (128, 512),
    "middle_pivot": (256, 512),
    "root_pivot": (256, 256),
}


def halves(value):
    high = value.astype(BF16)
    return high, (value - high.astype(F32)).astype(BF16)


def product(vector, high, low, contract):
    vector_high, vector_low = halves(vector)
    dims = (((1,), (contract,)), ((), ()))
    both = lax.dot_general(
        jnp.concatenate([vector_high, vector_low], axis=0), high, dims, preferred_element_type=F32
    )
    rest = lax.dot_general(vector_high, low, dims, preferred_element_type=F32)
    return both[:16] + (both[16:] + rest)


def pick(selector, blocks):
    high, low = halves(blocks)
    return jnp.dot(selector, high, preferred_element_type=F32) + jnp.dot(
        selector, low, preferred_element_type=F32
    )


def as_float(condition):
    return jnp.where(condition, 1.0, 0.0).astype(BF16)


def flipped(selector):
    count = selector.shape[1]
    rows = lax.broadcasted_iota(jnp.int32, (count, count), 0)
    cols = lax.broadcasted_iota(jnp.int32, (count, count), 1)
    return lax.dot_general(
        as_float(rows == cols), selector, (((1,), (1,)), ((), ())), preferred_element_type=F32
    ).astype(BF16)


def root_numbers(width):
    slot = lax.broadcasted_iota(jnp.int32, (64, width), 0)
    return (slot & 1) * 32 + (slot >> 1)


def group_numbers(width):
    slot = lax.broadcasted_iota(jnp.int32, (64, width), 0)
    return (slot & 3) * 16 + (slot >> 2)


def kernel(
    leaf_source,
    leaf_targets,
    root_source,
    middle_source,
    lower_source,
    middle_targets,
    lower_targets,
    *rest,
):
    in_hbm = dict(zip(MATRICES, rest[:7]))
    root_solution, middle_solution, lower_solution, leaf_solution = rest[7:11]
    rest = rest[11:]
    loaded = dict(zip(MATRICES, rest[:7]))
    high = dict(zip(MATRICES, rest[7:14]))
    low = dict(zip(MATRICES, rest[14:21]))
    rest = rest[21:]
    out_of = dict(zip(NAMES, rest[: len(NAMES)]))
    into = dict(zip(NAMES, rest[len(NAMES) : 2 * len(NAMES)]))
    send_sem, recv_sem, load_sem = rest[2 * len(NAMES) :]

    r = lax.axis_index("row")
    c = lax.axis_index("col")
    half = c // 16
    i16 = r % 16
    j16 = c % 16
    y, x, core = c // 8, (c // 2) % 4, c % 2
    my_place = {"row16": i16, "row32": r, "col16": j16, "col32": c}

    def peer(kind, step):
        if kind == "row32":
            odd = step % 2
            place = (r + 16 + (2 * odd - 1) * ((step + 1) // 2)) % 32
            return place, (place, c)
        if kind == "row16":
            back = i16 // 8
            own = i16 * back + (15 - i16) * (1 - back)
            at = step + jnp.where(step >= own, 1, 0)
            place = at * back + (15 - at) * (1 - back)
            return place, (r - i16 + place, c)
        if kind == "col16":
            at = step + jnp.where(step >= 13, 1, 0)
            there_y = (y % 2 + 1 + at // 8) % 2
            there_x = (x + 2 + at // 2) % 4
            there_core = (core + 1 + at) % 2
            place = there_y * 8 + there_x * 2 + there_core
            return place, (r, half * 16 + place)
        at = step + jnp.where(step >= 21, 1, 0)
        there_y = (y + 2 + at // 8) % 4
        there_x = (x + 2 + at // 2) % 4
        there_core = (core + 1 + at) % 2
        place = there_y * 8 + there_x * 2 + there_core
        return place, (r, place)

    def send(name, each=None):
        kind, rows = PHASES[name]
        index = NAMES.index(name)
        source, target = out_of[name], into[name]

        def piece(place):
            return source.at[pl.ds(0 if each is None else each(place) * rows, rows)]

        here = target.at[pl.ds(my_place[kind] * rows, rows)]

        def one(step, carry):
            place, device = peer(kind, step)
            pltpu.make_async_remote_copy(
                src_ref=piece(place),
                dst_ref=here,
                send_sem=send_sem.at[index],
                recv_sem=recv_sem.at[index],
                device_id=device,
                device_id_type=MESH,
            ).start()
            return carry

        lax.fori_loop(0, COUNT[kind] - 1, one, 0)
        pltpu.make_async_copy(piece(my_place[kind]), here, recv_sem.at[index]).start()

    def arrived(name):
        buffer = into[name]
        pltpu.make_async_copy(buffer, buffer, recv_sem.at[NAMES.index(name)]).wait()
        return buffer

    def total(name):
        kind, rows = PHASES[name]
        buffer = arrived(name)
        parts = [buffer[pl.ds(8 * at, 8), :] for at in range(COUNT[kind] * rows // 8)]
        while len(parts) > 1:
            parts = [a + b for a, b in zip(parts[::2], parts[1::2])]
        value = parts[0]
        size = 8
        while size > rows:
            size //= 2
            value = value[:size] + value[size:]
        return value

    def wide(buffer, rows, start=0):
        return jnp.concatenate(
            [buffer[pl.ds(start + at, 16, stride=rows), :] for at in range(rows)], axis=1
        )

    def put(name, value):
        rows = value.shape[1] // 128
        buffer = out_of[name]
        if rows == 1:
            buffer[...] = value
        else:
            for at in range(rows):
                buffer[pl.ds(at, 16, stride=rows), :] = value[:, at * 128 : (at + 1) * 128]

    def stacked(name, value):
        for at in range(value.shape[1] // 128):
            out_of[name][pl.ds(at * 16, 16), :] = value[:, at * 128 : (at + 1) * 128]

    def load(name):
        index = list(MATRICES).index(name)
        return pltpu.make_async_copy(in_hbm[name], loaded[name], load_sem.at[index])

    def split(name):
        load(name).wait()
        high[name][...], low[name][...] = halves(loaded[name][...])

    def apply(name, vector):
        return product(vector, high[name][...], low[name][...], 1)

    def apply_transposed(name, vector):
        return product(vector, high[name][...], low[name][...], 0)

    same = lambda place: place

    for name in MATRICES:
        load(name).start()

    barrier = pltpu.get_barrier_semaphore()
    for kind in ("row32", "col32"):

        def greet(step, carry, kind=kind):
            pl.semaphore_signal(
                barrier, inc=1, device_id=peer(kind, step)[1], device_id_type=MESH
            )
            return carry

        lax.fori_loop(0, 31, greet, 0)

    lane = lax.broadcasted_iota(jnp.int32, (1, 128), 1)
    own_row = jnp.zeros((1, 128), F32)
    for m in range(4):
        own_row = jnp.where(lane == 4 * i16 + m, leaf_targets[0, 0, m].astype(F32), own_row)
    out_of["targets"][...] = own_row
    mid_src = middle_source[0, 0]
    out_of["middle_source"][...] = jnp.concatenate(
        [
            jnp.concatenate([mid_src[0:1], mid_src[1:2]], axis=1),
            jnp.concatenate([mid_src[2:3], mid_src[3:4]], axis=1),
        ],
        axis=0,
    )
    root_src = root_source[0, 0]
    out_of["root_source"][...] = jnp.concatenate([root_src[0:1], root_src[1:2]], axis=1)

    leaf_vector = jnp.concatenate([leaf_source[0, 0, 0], leaf_source[0, 0, 1]], axis=1)
    split("leaf_update")
    put("leaf_send", apply("leaf_update", leaf_vector))

    pl.semaphore_wait(barrier, 62)
    send("targets")
    send("leaf_send", same)
    send("middle_source")
    send("root_source")

    for name in list(MATRICES)[1:]:
        split(name)
    leaf_terms = apply_transposed("leaf_pivot", apply("leaf_pivot", leaf_vector))

    mid_target = middle_targets[pl.ds(half, 1), :]
    mid_place = as_float(root_numbers(32) == mid_target)
    mid_place_flip = flipped(mid_place)
    update_row = lax.broadcasted_iota(jnp.int32, (32, 64), 0)
    slot = lax.broadcasted_iota(jnp.int32, (32, 64), 1)
    order = (update_row & 15) * 2 + (update_row >> 4)
    low_target = jnp.zeros((8, 64), F32)
    for part in range(2):
        values = lower_targets[pl.ds(2 * half + part, 1), :].astype(F32)
        low_target = low_target + jnp.dot(
            jnp.broadcast_to(values, (8, 32)).astype(BF16),
            as_float(slot == order + 32 * part),
            preferred_element_type=F32,
        )
    low_target = low_target[0:1]
    low_place_root = as_float(root_numbers(64).astype(F32) == low_target)
    low_place_mid = as_float((group_numbers(64) + 64).astype(F32) == low_target)
    low_place_root_flip = flipped(low_place_root)
    low_place_mid_flip = flipped(low_place_mid)

    leaf_target = jnp.sum(arrived("targets")[...], axis=0, keepdims=True)[:, :64]
    leaf_place_low = as_float((group_numbers(64) + 128).astype(F32) == leaf_target)
    sent = arrived("leaf_send")[...]
    out_of["low_sum"][...] = pick(leaf_place_low, sent)
    send("low_sum", same)
    leaf_place_mid = as_float((group_numbers(64) + 64).astype(F32) == leaf_target)
    leaf_place_root = as_float(root_numbers(64).astype(F32) == leaf_target)
    out_of["mid_sum"][...] = pick(leaf_place_mid, sent)
    send("mid_sum", same)

    out_of["low_input"][...] = lower_source[0, 0] - total("low_sum")
    send("low_input")
    out_of["root_sum"][...] = pick(leaf_place_root, sent)
    send("root_sum", same)
    out_of["mid_base"][...] = total("mid_sum")
    send("mid_base")
    leaf_place_low_flip = flipped(leaf_place_low)
    leaf_place_mid_flip = flipped(leaf_place_mid)
    leaf_place_root_flip = flipped(leaf_place_root)
    out_of["root_base"][...] = total("root_sum")

    low_vector = wide(arrived("low_input"), 4)
    put("low_update", apply("lower_update", low_vector))
    send("low_update", same)
    put("low_product", apply("lower_pivot", low_vector))
    out_of["low_spread"][...] = total("low_update")
    send("low_spread")
    send("low_product", same)
    send("root_base")
    out_of["low_forward"][...] = total("low_product")
    send("low_forward")
    upper_lane = lax.broadcasted_iota(jnp.int32, (16, 128), 1) >= 64
    source_rows = arrived("middle_source")
    mid_base = []
    for pair in range(2):
        even = source_rows[pl.ds(pair, 16, stride=4), :]
        odd = source_rows[pl.ds(2 + pair, 16, stride=4), :]
        mid_base.append(jnp.where(upper_lane, pltpu.roll(odd, 64, 1), even))
        mid_base.append(jnp.where(upper_lane, odd, pltpu.roll(even, 64, 1)))
    sums = arrived("mid_base")
    mid_base = jnp.concatenate(mid_base, axis=1) - (wide(sums, 4) + wide(sums, 4, 64))
    low_terms = apply_transposed("lower_pivot", wide(arrived("low_forward"), 4))

    updates = arrived("low_spread")[...]
    out_of["mid_input"][...] = pick(low_place_mid, updates)
    send("mid_input", same)
    root_updates = pick(low_place_root, updates)
    mid_vector = mid_base - wide(arrived("mid_input"), 4)
    put("mid_update", apply("middle_update", mid_vector))
    send("mid_update", same)
    put("mid_product", apply("middle_pivot", mid_vector))
    out_of["mid_spread"][...] = total("mid_update")
    send("mid_spread")
    send("mid_product", same)
    out_of["mid_forward"][...] = total("mid_product")
    send("mid_forward")
    source_rows = arrived("root_source")
    even = source_rows[pl.ds(0, 16, stride=2), :]
    odd = source_rows[pl.ds(1, 16, stride=2), :]
    root_base = jnp.concatenate(
        [
            jnp.where(upper_lane, pltpu.roll(odd, 64, 1), even),
            jnp.where(upper_lane, odd, pltpu.roll(even, 64, 1)),
        ],
        axis=1,
    )
    sums = arrived("root_base")
    root_base = root_base - (wide(sums, 2) + wide(sums, 2, 32))
    mid_terms = apply_transposed("middle_pivot", wide(arrived("mid_forward"), 2))

    out_of["root_input"][...] = root_updates + pick(mid_place, arrived("mid_spread")[...])
    send("root_input", same)
    sums = arrived("root_input")
    root_vector = root_base - (wide(sums, 2) + wide(sums, 2, 32))
    stacked("root_product", apply("root_pivot", root_vector))
    send("root_product", same)
    out_of["root_forward"][...] = total("root_product")
    send("root_forward")
    forward = arrived("root_forward")
    forward = jnp.concatenate([forward[pl.ds(0, 16), :], forward[pl.ds(16, 16), :]], axis=1)
    terms = apply_transposed("root_pivot", forward)
    put("root_terms", terms)
    send("root_terms", lambda place: place % 16)
    stacked("root_rows", terms)
    send("root_rows", same)

    root_blocks = arrived("root_terms")[...]
    out_of["mid_fetch"][...] = pick(mid_place_flip, root_blocks)
    send("mid_fetch", same)
    low_root_part = pick(low_place_root_flip, root_blocks)
    out_of["root_out"][...] = total("root_rows")
    send("root_out")
    out_of["mid_fetched"][...] = total("mid_fetch")
    send("mid_fetched")
    terms = mid_terms - apply_transposed("middle_update", arrived("mid_fetched")[...])
    put("mid_terms", terms)
    send("mid_terms", same)
    for high_part in range(2):
        for low_part in range(2):
            at = (2 * high_part + low_part) * 128
            out_of["mid_rows"][pl.ds(32 * high_part + low_part, 16, stride=2), :] = terms[
                :, at : at + 128
            ]
    send("mid_rows", same)

    out_of["low_fetch"][...] = low_root_part + pick(
        low_place_mid_flip, arrived("mid_terms")[...]
    )
    send("low_fetch", same)
    done = arrived("root_out")
    chosen = lax.broadcasted_iota(jnp.int32, (16, 128), 0) == i16
    for q in range(2):
        block = done[pl.ds(16 * q, 16), :]
        root_solution[0, 0, q] = block
        out_of["root_chain"][pl.ds(q, 1), :] = jnp.sum(
            jnp.where(chosen, block, 0.0), axis=0, keepdims=True
        )
    send("root_chain")
    out_of["mid_out"][...] = total("mid_rows")
    send("mid_out")
    leaf_part = pick(leaf_place_root_flip, arrived("root_chain")[...])
    out_of["low_fetched"][...] = total("low_fetch")
    send("low_fetched")
    terms = low_terms - apply_transposed("lower_update", wide(arrived("low_fetched"), 2))
    put("low_rows", terms)
    send("low_rows", same)
    done = arrived("mid_out")
    for q in range(4):
        block = done[pl.ds(32 * (q // 2) + q % 2, 16, stride=2), :]
        middle_solution[0, 0, q] = block
        out_of["mid_chain"][pl.ds(q, 1), :] = jnp.sum(
            jnp.where(chosen, block, 0.0), axis=0, keepdims=True
        )
    send("mid_chain")
    leaf_part = leaf_part + pick(leaf_place_mid_flip, arrived("mid_chain")[...])

    finished = total("low_rows")
    out_of["low_chain"][...] = finished
    send("low_chain")
    out_of["low_out"][...] = finished
    send("low_out")
    out_of["leaf_fetch"][...] = leaf_part + pick(
        leaf_place_low_flip, arrived("low_chain")[...]
    )
    send("leaf_fetch", same)
    done = arrived("low_out")
    for q in range(4):
        lower_solution[0, 0, q] = done[pl.ds(q, 16, stride=4), :]
    answer = leaf_terms - apply_transposed("leaf_update", wide(arrived("leaf_fetch"), 4))
    leaf_solution[0, 0, 0] = answer[:, :128]
    leaf_solution[0, 0, 1] = answer[:, 128:]

    for index, name in enumerate(NAMES):
        kind, rows = PHASES[name]
        gone = into[name].at[pl.ds(0, (COUNT[kind] - 1) * rows)]
        pltpu.make_async_copy(gone, gone, send_sem.at[index]).wait()


def local(
    leaf_source,
    leaf_pivot,
    leaf_update,
    leaf_targets,
    root_source,
    middle_source,
    lower_source,
    root_pivot,
    middle_pivot,
    lower_pivot,
    middle_update,
    lower_update,
    middle_targets,
    lower_targets,
):
    matrices = {
        "leaf_update": leaf_update,
        "leaf_pivot": leaf_pivot,
        "lower_update": lower_update,
        "lower_pivot": lower_pivot,
        "middle_update": middle_update,
        "middle_pivot": middle_pivot,
        "root_pivot": root_pivot,
    }
    in_vmem = pl.BlockSpec(memory_space=pltpu.VMEM)
    in_smem = pl.BlockSpec(memory_space=pltpu.SMEM)
    anywhere = pl.BlockSpec(memory_space=pl.ANY)
    shapes = list(MATRICES.values())
    return pl.pallas_call(
        kernel,
        out_shape=tuple(
            jax.ShapeDtypeStruct((1, 1, blocks, 16, 128), F32) for blocks in (2, 4, 4, 2)
        ),
        in_specs=[in_vmem, in_smem] + [in_vmem] * 5 + [anywhere] * 7,
        out_specs=(in_vmem,) * 4,
        scratch_shapes=[pltpu.VMEM(shape, F32) for shape in shapes]
        + [pltpu.VMEM(shape, BF16) for shape in shapes] * 2
        + [pltpu.VMEM((SOURCES_OF[name], 128), F32) for name in NAMES]
        + [pltpu.VMEM((COUNT[PHASES[name][0]] * PHASES[name][1], 128), F32) for name in NAMES]
        + [
            pltpu.SemaphoreType.DMA((len(NAMES),)),
            pltpu.SemaphoreType.DMA((len(NAMES),)),
            pltpu.SemaphoreType.DMA((7,)),
        ],
        compiler_params=pltpu.CompilerParams(
            collective_id=0, has_side_effects=True, vmem_limit_bytes=40 * 1024 * 1024
        ),
    )(
        leaf_source,
        leaf_targets,
        root_source,
        middle_source,
        lower_source,
        middle_targets,
        lower_targets,
        *[matrices[name] for name in MATRICES],
    )


def solution(mesh):
    placed = (
        P("row", "col", None, None, None),
        P("row", "col"),
        P("row", "col"),
        P("row", "col", None),
        P("row", "col", None, None),
        P("row", "col", None, None),
        P("row", "col", None, None),
        P("row", "col"),
        P("row", "col"),
        P("row", "col"),
        P("row", "col"),
        P("row", "col"),
        P(),
        P(),
    )
    return jax.shard_map(
        local,
        mesh=mesh,
        in_specs=placed,
        out_specs=(P("row", "col", None, None, None),) * 4,
        check_vma=False,
    )
```

```python
import jax
import jax.numpy as jnp
from jax import lax
from jax.experimental import pallas as pl
from jax.experimental.pallas import tpu as pltpu
from jax.sharding import PartitionSpec as P

MESH = pl.DeviceIdType.MESH
F32 = jnp.float32
BF16 = jnp.bfloat16

ROW16, ROW32, COL16, COL32, INWARD, OUTWARD, OUTWARD_ALL = range(7)
(
    TARGETS,
    LEAF_SEND,
    MIDDLE_SOURCE,
    ROOT_SOURCE,
    LOW_BASE,
    LOW_SUM,
    MID_SUM,
    ROOT_SUM,
    LOW_INPUT,
    MID_BASE,
    ROOT_BASE,
    LOW_UPDATE,
    LOW_PRODUCT,
    LOW_FORWARD,
    LOW_SPREAD,
    MID_INPUT,
    MID_UPDATE,
    MID_PRODUCT,
    MID_FORWARD,
    MID_SPREAD,
    ROOT_INPUT,
    ROOT_PRODUCT,
    ROOT_FORWARD,
    ROOT_TERMS,
    MID_FETCH,
    MID_FETCHED,
    ROOT_ROWS,
    ROOT_OUT,
    ROOT_CHAIN,
    MID_TERMS,
    LOW_FETCH,
    LOW_FETCHED,
    MID_ROWS,
    MID_OUT,
    MID_CHAIN,
    LOW_ROWS,
    LOW_CHAIN,
    LOW_OUT,
    LEAF_FETCH,
) = range(39)
(
    LEAF_UPDATE_TILE,
    LEAF_PIVOT_TILE,
    LOWER_UPDATE_TILE,
    LOWER_PIVOT_TILE,
    MIDDLE_UPDATE_TILE,
    MIDDLE_PIVOT_TILE,
    ROOT_PIVOT_TILE,
) = range(7)

PHASES = {
    TARGETS: (ROW16, 1),
    LEAF_SEND: (INWARD, 8),
    MIDDLE_SOURCE: (ROW32, 2),
    ROOT_SOURCE: (ROW32, 1),
    LOW_BASE: (ROW16, 4),
    LOW_SUM: (COL16, 8),
    MID_SUM: (COL16, 8),
    ROOT_SUM: (COL32, 4),
    LOW_INPUT: (OUTWARD, 8),
    MID_BASE: (OUTWARD_ALL, 8),
    ROOT_BASE: (OUTWARD_ALL, 4),
    LOW_UPDATE: (COL16, 2),
    LOW_PRODUCT: (COL16, 4),
    LOW_FORWARD: (COL16, 4),
    LOW_SPREAD: (ROW32, 2),
    MID_INPUT: (COL16, 4),
    MID_UPDATE: (COL16, 1),
    MID_PRODUCT: (COL16, 2),
    MID_FORWARD: (COL16, 2),
    MID_SPREAD: (ROW32, 1),
    ROOT_INPUT: (COL32, 2),
    ROOT_PRODUCT: (COL32, 1),
    ROOT_FORWARD: (COL32, 1),
    ROOT_TERMS: (COL32, 2),
    MID_FETCH: (ROW32, 1),
    MID_FETCHED: (COL16, 1),
    ROOT_ROWS: (ROW32, 1),
    ROOT_OUT: (ROW32, 1),
    ROOT_CHAIN: (COL32, 4),
    MID_TERMS: (COL16, 4),
    LOW_FETCH: (ROW32, 2),
    LOW_FETCHED: (COL16, 2),
    MID_ROWS: (ROW32, 2),
    MID_OUT: (ROW32, 2),
    MID_CHAIN: (COL16, 8),
    LOW_ROWS: (INWARD, 8),
    LOW_CHAIN: (COL16, 8),
    LOW_OUT: (OUTWARD, 8),
    LEAF_FETCH: (OUTWARD, 8),
}
NAMES = list(PHASES)
COUNT = {ROW16: 16, ROW32: 32, COL16: 16, COL32: 32, INWARD: 16, OUTWARD: 8, OUTWARD_ALL: 16}
CENTRAL = (LOW_SUM, MID_SUM, ROOT_SUM, ROOT_CHAIN, MID_CHAIN, LOW_CHAIN)

SOURCES_OF = {
    TARGETS: 1,
    LEAF_SEND: 64,
    MIDDLE_SOURCE: 2,
    ROOT_SOURCE: 1,
    LOW_BASE: 4,
    LOW_SUM: 128,
    MID_SUM: 128,
    ROOT_SUM: 128,
    LOW_INPUT: 8,
    MID_BASE: 8,
    ROOT_BASE: 4,
    LOW_UPDATE: 32,
    LOW_PRODUCT: 64,
    LOW_FORWARD: 4,
    LOW_SPREAD: 2,
    MID_INPUT: 64,
    MID_UPDATE: 16,
    MID_PRODUCT: 32,
    MID_FORWARD: 2,
    MID_SPREAD: 1,
    ROOT_INPUT: 64,
    ROOT_PRODUCT: 32,
    ROOT_FORWARD: 1,
    ROOT_TERMS: 32,
    MID_FETCH: 32,
    MID_FETCHED: 1,
    ROOT_ROWS: 32,
    ROOT_OUT: 1,
    ROOT_CHAIN: 4,
    MID_TERMS: 64,
    LOW_FETCH: 64,
    LOW_FETCHED: 2,
    MID_ROWS: 64,
    MID_OUT: 2,
    MID_CHAIN: 8,
    LOW_ROWS: 64,
    LOW_CHAIN: 8,
    LOW_OUT: 8,
    LEAF_FETCH: 128,
}

MATRICES = {
    LEAF_UPDATE_TILE: (512, 256),
    LEAF_PIVOT_TILE: (256, 256),
    LOWER_UPDATE_TILE: (256, 512),
    LOWER_PIVOT_TILE: (512, 512),
    MIDDLE_UPDATE_TILE: (128, 512),
    MIDDLE_PIVOT_TILE: (256, 512),
    ROOT_PIVOT_TILE: (256, 256),
}


def halves(value):
    high = value.astype(BF16)
    return high, (value - high.astype(F32)).astype(BF16)


def product(vector, high, low, contract):
    vector_high, vector_low = halves(vector)
    dims = (((1,), (contract,)), ((), ()))
    both = lax.dot_general(
        jnp.concatenate([vector_high, vector_low], axis=0), high, dims, preferred_element_type=F32
    )
    rest = lax.dot_general(vector_high, low, dims, preferred_element_type=F32)
    return both[:16] + (both[16:] + rest)


def pick(selector, blocks):
    high, low = halves(blocks)
    return jnp.dot(selector, high, preferred_element_type=F32) + jnp.dot(
        selector, low, preferred_element_type=F32
    )


def as_float(condition):
    return jnp.where(condition, 1.0, 0.0).astype(BF16)


def flipped(selector):
    count = selector.shape[1]
    rows = lax.broadcasted_iota(jnp.int32, (count, count), 0)
    cols = lax.broadcasted_iota(jnp.int32, (count, count), 1)
    return lax.dot_general(
        as_float(rows == cols), selector, (((1,), (1,)), ((), ())), preferred_element_type=F32
    ).astype(BF16)


def root_numbers(width):
    slot = lax.broadcasted_iota(jnp.int32, (64, width), 0)
    return (slot & 1) * 32 + (slot >> 1)


def group_numbers(width):
    slot = lax.broadcasted_iota(jnp.int32, (64, width), 0)
    return (slot & 3) * 16 + (slot >> 2)


def kernel(*rest):
    small_hbm = rest[:7]
    in_hbm = dict(zip(MATRICES, rest[7:14]))
    root_solution, middle_solution, lower_solution, leaf_solution = rest[14:18]
    small = rest[18:25]
    leaf_source, leaf_targets, root_source, middle_source, lower_source = small[:5]
    middle_targets, lower_targets = small[5:]
    rest = rest[25:]
    loaded = dict(zip(MATRICES, rest[:7]))
    high = dict(zip(MATRICES, rest[7:14]))
    low = dict(zip(MATRICES, rest[14:21]))
    rest = rest[21:]
    out_of = dict(zip(NAMES, rest[: len(NAMES)]))
    into = dict(zip(NAMES, rest[len(NAMES) : 2 * len(NAMES)]))
    tally, send_sem, recv_sem, load_sem = rest[2 * len(NAMES) :]

    r = lax.axis_index("row")
    c = lax.axis_index("col")
    half = c // 16
    i16 = r % 16
    j16 = c % 16
    core, x, y = lax.rem(c, 2), lax.rem(c // 2, 4), c // 8
    low_y = lax.rem(y, 2)
    back = i16 // 8
    own = i16 * back + (15 - i16) * (1 - back)
    central = jnp.logical_and(i16 >= 4, i16 < 12)
    my_place = {ROW16: i16, ROW32: r, COL16: j16, COL32: c}

    def peer(kind, step):
        if kind == ROW32:
            odd = lax.rem(step, 2)
            place = lax.rem(r + 16 + (2 * odd - 1) * lax.div(step + 1, 2), 32)
            return place, (place, c)
        if kind == ROW16:
            at = step + jnp.where(step >= own, 1, 0)
            place = at * back + (15 - at) * (1 - back)
            return place, (r - i16 + place, c)
        if kind == COL16:
            at = step + jnp.where(step >= 13, 1, 0)
            place = (
                lax.rem(low_y + 1 + lax.div(at, 8), 2) * 8
                + lax.rem(x + 2 + lax.div(at, 2), 4) * 2
                + lax.rem(core + 1 + at, 2)
            )
            return place, (r, half * 16 + place)
        at = step + jnp.where(step >= 21, 1, 0)
        place = (
            lax.rem(y + 2 + lax.div(at, 8), 4) * 8
            + lax.rem(x + 2 + lax.div(at, 2), 4) * 2
            + lax.rem(core + 1 + at, 2)
        )
        return place, (r, place)

    def each_peer(kind, act):
        lax.fori_loop(0, COUNT[kind] - 1, act, 0)

    def send(name, each=None):
        kind, rows = PHASES[name]
        index = NAMES.index(name)
        source, target = out_of[name], into[name]

        def piece(place):
            return source.at[pl.ds(0 if each is None else each(place) * rows, rows)]

        here = target.at[pl.ds(my_place[kind] * rows, rows)]

        def one(step, carry):
            place, device = peer(kind, step)
            pltpu.make_async_remote_copy(
                src_ref=piece(place),
                dst_ref=here,
                send_sem=send_sem.at[index],
                recv_sem=recv_sem.at[index],
                device_id=device,
                device_id_type=MESH,
            ).start()
            return carry

        each_peer(kind, one)
        pltpu.make_async_copy(piece(my_place[kind]), here, recv_sem.at[index]).start()

    def remote(name, source, target, device):
        index = NAMES.index(name)
        pltpu.make_async_remote_copy(
            src_ref=source,
            dst_ref=target,
            send_sem=send_sem.at[index],
            recv_sem=recv_sem.at[index],
            device_id=device,
            device_id_type=MESH,
        ).start()

    def inward(name):
        source, target = out_of[name], into[name]
        here = target.at[pl.ds(i16 * 8, 8)]

        def one(step, carry):
            at = step * back + (7 - step) * (1 - back)

            @pl.when(at + 4 != i16)
            def _():
                remote(name, source.at[pl.ds(at * 8, 8)], here, (r - i16 + 4 + at, c))

            return carry

        lax.fori_loop(0, 8, one, 0)

        @pl.when(central)
        def _():
            pltpu.make_async_copy(
                source.at[pl.ds((i16 - 4) * 8, 8)], here, recv_sem.at[NAMES.index(name)]
            ).start()

    def outward(name, each=None):
        kind, rows = PHASES[name]
        source, target = out_of[name], into[name]

        def piece(place):
            return source.at[pl.ds(0 if each is None else each(place) * rows, rows)]

        if kind == OUTWARD_ALL:
            here = target.at[pl.ds((r // 16 * 8 + i16 - 4) * rows, rows)]

            def one(step, carry):
                place, device = peer(ROW32, step)
                remote(name, piece(place), here, device)
                return carry

            lax.fori_loop(0, 31, one, 0)
            own_piece = piece(r)
        else:
            here = target.at[pl.ds((i16 - 4) * rows, rows)]

            def one(step, carry):
                place, device = peer(ROW16, step)
                remote(name, piece(place), here, device)
                return carry

            lax.fori_loop(0, 15, one, 0)
            own_piece = piece(i16)
        pltpu.make_async_copy(own_piece, here, recv_sem.at[NAMES.index(name)]).start()

    def arrived(name):
        buffer = into[name]
        pltpu.make_async_copy(buffer, buffer, recv_sem.at[NAMES.index(name)]).wait()
        return buffer

    def total(name):
        kind, rows = PHASES[name]
        buffer = arrived(name)
        parts = [buffer[pl.ds(8 * at, 8), :] for at in range(COUNT[kind] * rows // 8)]
        while len(parts) > 1:
            parts = [a + b for a, b in zip(parts[::2], parts[1::2])]
        value = parts[0]
        size = 8
        while size > rows:
            size //= 2
            value = value[:size] + value[size:]
        return value

    def wide(buffer, rows, start=0):
        return jnp.concatenate(
            [buffer[pl.ds(start + at, 16, stride=rows), :] for at in range(rows)], axis=1
        )

    def put(name, value):
        rows = value.shape[1] // 128
        buffer = out_of[name]
        if rows == 1:
            buffer[...] = value
        else:
            for at in range(rows):
                buffer[pl.ds(at, 16, stride=rows), :] = value[:, at * 128 : (at + 1) * 128]

    def stacked(name, value):
        for at in range(value.shape[1] // 128):
            out_of[name][pl.ds(at * 16, 16), :] = value[:, at * 128 : (at + 1) * 128]

    def load(name):
        index = list(MATRICES).index(name)
        return pltpu.make_async_copy(in_hbm[name], loaded[name], load_sem.at[index])

    def split(name):
        load(name).wait()
        high[name][...], low[name][...] = halves(loaded[name][...])

    def apply(name, vector):
        return product(vector, high[name][...], low[name][...], 1)

    def apply_transposed(name, vector):
        return product(vector, high[name][...], low[name][...], 0)

    same = lambda place: place

    def load_small(index):
        return pltpu.make_async_copy(small_hbm[index], small[index], load_sem.at[7 + index])

    load_small(0).start()
    load_small(1).start()
    for name in MATRICES:
        load(name).start()
    for index in range(2, 7):
        load_small(index).start()

    barrier = pltpu.get_barrier_semaphore()
    for kind in (ROW32, COL32):

        def greet(step, carry, kind=kind):
            pl.semaphore_signal(
                barrier, inc=1, device_id=peer(kind, step)[1], device_id_type=MESH
            )
            return carry

        each_peer(kind, greet)

    for index in range(7):
        load_small(index).wait()
    lane = lax.broadcasted_iota(jnp.int32, (4, 128), 1)
    entry = lax.broadcasted_iota(jnp.int32, (4, 128), 0)
    own_lane = jnp.logical_and(lane >> 3 == i16, lane & 3 == entry)
    own_targets = jnp.broadcast_to(leaf_targets[0].astype(F32), (8, 4)).astype(BF16)
    out_of[TARGETS][...] = jnp.dot(
        own_targets, as_float(own_lane), preferred_element_type=F32
    )[0:1]
    mid_src = middle_source[0, 0]
    out_of[MIDDLE_SOURCE][...] = jnp.concatenate(
        [
            jnp.concatenate([mid_src[0:1], mid_src[1:2]], axis=1),
            jnp.concatenate([mid_src[2:3], mid_src[3:4]], axis=1),
        ],
        axis=0,
    )
    root_src = root_source[0, 0]
    out_of[ROOT_SOURCE][...] = jnp.concatenate([root_src[0:1], root_src[1:2]], axis=1)

    leaf_vector = jnp.concatenate([leaf_source[0, 0, 0], leaf_source[0, 0, 1]], axis=1)
    split(LEAF_UPDATE_TILE)
    put(LEAF_SEND, apply(LEAF_UPDATE_TILE, leaf_vector))

    pl.semaphore_wait(barrier, 62)
    inward(LEAF_SEND)
    send(TARGETS)
    out_of[LOW_BASE][...] = lower_source[0, 0]

    for name in list(MATRICES)[1:]:
        split(name)
    leaf_terms = apply_transposed(LEAF_PIVOT_TILE, apply(LEAF_PIVOT_TILE, leaf_vector))

    mid_target = middle_targets[pl.ds(half, 1), :]
    mid_place = as_float(root_numbers(32) == mid_target)
    mid_place_flip = flipped(mid_place)
    update_row = lax.broadcasted_iota(jnp.int32, (32, 64), 0)
    slot = lax.broadcasted_iota(jnp.int32, (32, 64), 1)
    order = (update_row & 15) * 2 + (update_row >> 4)
    low_target = jnp.zeros((8, 64), F32)
    for part in range(2):
        values = lower_targets[pl.ds(2 * half + part, 1), :].astype(F32)
        low_target = low_target + jnp.dot(
            jnp.broadcast_to(values, (8, 32)).astype(BF16),
            as_float(slot == order + 32 * part),
            preferred_element_type=F32,
        )
    low_target = low_target[0:1]
    low_place_root = as_float(root_numbers(64).astype(F32) == low_target)
    low_place_mid = as_float((group_numbers(64) + 64).astype(F32) == low_target)
    low_place_root_flip = flipped(low_place_root)
    low_place_mid_flip = flipped(low_place_mid)

    send(LOW_BASE)

    lane = lax.broadcasted_iota(jnp.int32, (1, 128), 1)
    leaf_target = jnp.sum(arrived(TARGETS)[...], axis=0, keepdims=True)
    leaf_target = leaf_target + ((lane >> 2 & 1) * 256).astype(F32)
    slot = lax.broadcasted_iota(jnp.int32, (128, 128), 0)
    group_number = (slot & 3) * 16 + (slot >> 3) + (slot >> 2 & 1) * 256
    root_number = (slot & 1) * 32 + (slot >> 2) + (slot >> 1 & 1) * 256
    leaf_place_low = as_float((group_number + 128).astype(F32) == leaf_target)
    leaf_place_mid = as_float((group_number + 64).astype(F32) == leaf_target)
    leaf_place_root = as_float(root_number.astype(F32) == leaf_target)

    @pl.when(central)
    def _():
        sent = arrived(LEAF_SEND)[...]
        out_of[LOW_SUM][...] = pick(leaf_place_low, sent)
        send(LOW_SUM, same)
        out_of[MID_SUM][...] = pick(leaf_place_mid, sent)
        send(MID_SUM, same)
        out_of[LOW_INPUT][...] = total(LOW_SUM)
        outward(LOW_INPUT)
        out_of[ROOT_SUM][...] = pick(leaf_place_root, sent)
        send(ROOT_SUM, same)
        out_of[MID_BASE][...] = total(MID_SUM)
        outward(MID_BASE)
        out_of[ROOT_BASE][...] = total(ROOT_SUM)

    leaf_place_low_flip = flipped(leaf_place_low)
    leaf_place_mid_flip = flipped(leaf_place_mid)
    leaf_place_root_flip = flipped(leaf_place_root)

    low_base = wide(arrived(LOW_BASE), 4)
    low_vector = low_base - wide(arrived(LOW_INPUT), 4)
    put(LOW_UPDATE, apply(LOWER_UPDATE_TILE, low_vector))
    send(LOW_UPDATE, same)
    send(MIDDLE_SOURCE)
    put(LOW_PRODUCT, apply(LOWER_PIVOT_TILE, low_vector))
    out_of[LOW_SPREAD][...] = total(LOW_UPDATE)
    send(LOW_SPREAD)
    send(LOW_PRODUCT, same)
    out_of[LOW_FORWARD][...] = total(LOW_PRODUCT)
    send(LOW_FORWARD)
    upper_lane = lax.broadcasted_iota(jnp.int32, (16, 128), 1) >= 64
    source_rows = arrived(MIDDLE_SOURCE)
    mid_base = []
    for pair in range(2):
        even = source_rows[pl.ds(pair, 16, stride=4), :]
        odd = source_rows[pl.ds(2 + pair, 16, stride=4), :]
        mid_base.append(jnp.where(upper_lane, pltpu.roll(odd, 64, 1), even))
        mid_base.append(jnp.where(upper_lane, odd, pltpu.roll(even, 64, 1)))
    sums = arrived(MID_BASE)
    mid_base = jnp.concatenate(mid_base, axis=1) - (wide(sums, 4) + wide(sums, 4, 64))
    low_terms = apply_transposed(LOWER_PIVOT_TILE, wide(arrived(LOW_FORWARD), 4))

    updates = arrived(LOW_SPREAD)[...]
    out_of[MID_INPUT][...] = pick(low_place_mid, updates)
    send(MID_INPUT, same)

    @pl.when(central)
    def _():
        outward(ROOT_BASE)

    send(ROOT_SOURCE)
    root_updates = pick(low_place_root, updates)
    mid_vector = mid_base - wide(arrived(MID_INPUT), 4)
    put(MID_UPDATE, apply(MIDDLE_UPDATE_TILE, mid_vector))
    send(MID_UPDATE, same)
    put(MID_PRODUCT, apply(MIDDLE_PIVOT_TILE, mid_vector))
    out_of[MID_SPREAD][...] = total(MID_UPDATE)
    send(MID_SPREAD)
    send(MID_PRODUCT, same)
    out_of[MID_FORWARD][...] = total(MID_PRODUCT)
    send(MID_FORWARD)
    source_rows = arrived(ROOT_SOURCE)
    even = source_rows[pl.ds(0, 16, stride=2), :]
    odd = source_rows[pl.ds(1, 16, stride=2), :]
    root_base = jnp.concatenate(
        [
            jnp.where(upper_lane, pltpu.roll(odd, 64, 1), even),
            jnp.where(upper_lane, odd, pltpu.roll(even, 64, 1)),
        ],
        axis=1,
    )
    sums = arrived(ROOT_BASE)
    root_base = root_base - (wide(sums, 2) + wide(sums, 2, 32))
    mid_terms = apply_transposed(MIDDLE_PIVOT_TILE, wide(arrived(MID_FORWARD), 2))

    out_of[ROOT_INPUT][...] = root_updates + pick(mid_place, arrived(MID_SPREAD)[...])
    send(ROOT_INPUT, same)
    sums = arrived(ROOT_INPUT)
    root_vector = root_base - (wide(sums, 2) + wide(sums, 2, 32))
    stacked(ROOT_PRODUCT, apply(ROOT_PIVOT_TILE, root_vector))
    send(ROOT_PRODUCT, same)
    out_of[ROOT_FORWARD][...] = total(ROOT_PRODUCT)
    send(ROOT_FORWARD)
    forward = arrived(ROOT_FORWARD)
    forward = jnp.concatenate([forward[pl.ds(0, 16), :], forward[pl.ds(16, 16), :]], axis=1)
    terms = apply_transposed(ROOT_PIVOT_TILE, forward)
    put(ROOT_TERMS, terms)
    send(ROOT_TERMS, lambda place: place % 16)
    stacked(ROOT_ROWS, terms)
    send(ROOT_ROWS, same)

    root_blocks = arrived(ROOT_TERMS)[...]
    out_of[MID_FETCH][...] = pick(mid_place_flip, root_blocks)
    send(MID_FETCH, same)
    low_root_part = pick(low_place_root_flip, root_blocks)
    out_of[ROOT_OUT][...] = total(ROOT_ROWS)
    send(ROOT_OUT)
    out_of[MID_FETCHED][...] = total(MID_FETCH)
    send(MID_FETCHED)
    terms = mid_terms - apply_transposed(MIDDLE_UPDATE_TILE, arrived(MID_FETCHED)[...])
    put(MID_TERMS, terms)
    send(MID_TERMS, same)
    for high_part in range(2):
        for low_part in range(2):
            at = (2 * high_part + low_part) * 128
            out_of[MID_ROWS][pl.ds(32 * high_part + low_part, 16, stride=2), :] = terms[
                :, at : at + 128
            ]
    send(MID_ROWS, same)

    out_of[LOW_FETCH][...] = low_root_part + pick(
        low_place_mid_flip, arrived(MID_TERMS)[...]
    )
    send(LOW_FETCH, same)
    done = arrived(ROOT_OUT)
    row_number = lax.broadcasted_iota(jnp.int32, (16, 128), 0)
    for q in range(2):
        root_solution[0, 0, q] = done[pl.ds(16 * q, 16), :]

    def own_source(block, which):
        chosen = row_number == 2 * (i16 - 4) + which
        return jnp.sum(jnp.where(chosen, block, 0.0), axis=0, keepdims=True)

    @pl.when(central)
    def _():
        for q in range(2):
            for which in range(2):
                out_of[ROOT_CHAIN][pl.ds(2 * which + q, 1), :] = own_source(
                    into[ROOT_OUT][pl.ds(16 * q, 16), :], which
                )
        send(ROOT_CHAIN)

    out_of[MID_OUT][...] = total(MID_ROWS)
    send(MID_OUT)

    @pl.when(central)
    def _():
        out_of[LEAF_FETCH][...] = pick(leaf_place_root_flip, arrived(ROOT_CHAIN)[...])

    out_of[LOW_FETCHED][...] = total(LOW_FETCH)
    send(LOW_FETCHED)
    terms = low_terms - apply_transposed(LOWER_UPDATE_TILE, wide(arrived(LOW_FETCHED), 2))
    put(LOW_ROWS, terms)
    inward(LOW_ROWS)
    done = arrived(MID_OUT)
    for q in range(4):
        middle_solution[0, 0, q] = done[pl.ds(32 * (q // 2) + q % 2, 16, stride=2), :]

    @pl.when(central)
    def _():
        for q in range(4):
            for which in range(2):
                out_of[MID_CHAIN][pl.ds(4 * which + q, 1), :] = own_source(
                    into[MID_OUT][pl.ds(32 * (q // 2) + q % 2, 16, stride=2), :], which
                )
        send(MID_CHAIN)
        finished = total(LOW_ROWS)
        out_of[LOW_CHAIN][...] = finished
        send(LOW_CHAIN)
        out_of[LOW_OUT][...] = finished
        outward(LOW_OUT)
        out_of[LEAF_FETCH][...] += pick(leaf_place_mid_flip, arrived(MID_CHAIN)[...])
        out_of[LEAF_FETCH][...] += pick(leaf_place_low_flip, arrived(LOW_CHAIN)[...])
        outward(LEAF_FETCH, same)

    done = arrived(LOW_OUT)
    for q in range(4):
        lower_solution[0, 0, q] = done[pl.ds(q, 16, stride=4), :]
    answer = leaf_terms - apply_transposed(LEAF_UPDATE_TILE, wide(arrived(LEAF_FETCH), 4))
    leaf_solution[0, 0, 0] = answer[:, :128]
    leaf_solution[0, 0, 1] = answer[:, 128:]

    def gone(name, rows):
        buffer = tally.at[pl.ds(0, rows)]
        pltpu.make_async_copy(buffer, buffer, send_sem.at[NAMES.index(name)]).wait()

    for name in NAMES:
        kind, rows = PHASES[name]
        if kind not in (INWARD, OUTWARD, OUTWARD_ALL) and name not in CENTRAL:
            gone(name, (COUNT[kind] - 1) * rows)

    @pl.when(central)
    def _():
        for name in NAMES:
            kind, rows = PHASES[name]
            if name in CENTRAL:
                gone(name, (COUNT[kind] - 1) * rows)
            elif kind == INWARD:
                gone(name, 7 * rows)
            elif kind == OUTWARD:
                gone(name, 15 * rows)
            elif kind == OUTWARD_ALL:
                gone(name, 31 * rows)

    @pl.when(jnp.logical_not(central))
    def _():
        for name in NAMES:
            kind, rows = PHASES[name]
            if kind == INWARD:
                gone(name, 8 * rows)


def local(
    leaf_source,
    leaf_pivot,
    leaf_update,
    leaf_targets,
    root_source,
    middle_source,
    lower_source,
    root_pivot,
    middle_pivot,
    lower_pivot,
    middle_update,
    lower_update,
    middle_targets,
    lower_targets,
):
    matrices = {
        LEAF_UPDATE_TILE: leaf_update,
        LEAF_PIVOT_TILE: leaf_pivot,
        LOWER_UPDATE_TILE: lower_update,
        LOWER_PIVOT_TILE: lower_pivot,
        MIDDLE_UPDATE_TILE: middle_update,
        MIDDLE_PIVOT_TILE: middle_pivot,
        ROOT_PIVOT_TILE: root_pivot,
    }
    in_vmem = pl.BlockSpec(memory_space=pltpu.VMEM)
    in_hbm = pl.BlockSpec(memory_space=pltpu.HBM)
    small = (
        leaf_source,
        leaf_targets,
        root_source,
        middle_source,
        lower_source,
        middle_targets,
        lower_targets,
    )
    shapes = list(MATRICES.values())
    return pl.pallas_call(
        kernel,
        out_shape=tuple(
            jax.ShapeDtypeStruct((1, 1, blocks, 16, 128), F32) for blocks in (2, 4, 4, 2)
        ),
        in_specs=[in_hbm] * 14,
        out_specs=(in_vmem,) * 4,
        scratch_shapes=[pltpu.VMEM(array.shape, array.dtype) for array in small]
        + [pltpu.VMEM(shape, F32) for shape in shapes]
        + [pltpu.VMEM(shape, BF16) for shape in shapes] * 2
        + [pltpu.VMEM((SOURCES_OF[name], 128), F32) for name in NAMES]
        + [pltpu.VMEM((COUNT[PHASES[name][0]] * PHASES[name][1], 128), F32) for name in NAMES]
        + [
            pltpu.VMEM((256, 128), F32),
            pltpu.SemaphoreType.DMA((len(NAMES),)),
            pltpu.SemaphoreType.DMA((len(NAMES),)),
            pltpu.SemaphoreType.DMA((14,)),
        ],
        compiler_params=pltpu.CompilerParams(
            collective_id=0, has_side_effects=True, vmem_limit_bytes=60 * 1024 * 1024
        ),
    )(
        *small,
        *[matrices[name] for name in MATRICES],
    )


def solution(mesh):
    placed = (
        P("row", "col", None, None, None),
        P("row", "col"),
        P("row", "col"),
        P("row", "col", None),
        P("row", "col", None, None),
        P("row", "col", None, None),
        P("row", "col", None, None),
        P("row", "col"),
        P("row", "col"),
        P("row", "col"),
        P("row", "col"),
        P("row", "col"),
        P(),
        P(),
    )
    return jax.shard_map(
        local,
        mesh=mesh,
        in_specs=placed,
        out_specs=(P("row", "col", None, None, None),) * 4,
        check_vma=False,
    )
```
